512 devices in a mesh: copy: 2 (over y_hi), dp: 32 (over z, y_lo), vocab: 8 (over x, core).
Axes of the slice: x: 4, y: 4 (y_hi: 2, y_lo: 2; y = y_hi * 2 + y_lo), z: 16, core: 2. Of those that a mesh axis runs over, the one named last changes fastest.
Arguments:
- hidden: bfloat16 [2, 768, 4096], P('copy', ('dp', 'vocab')), may hold values from -6 to 6
- head_weight: bfloat16 [2, 4096, 65536], P('copy', None, ('dp', 'vocab')), may hold values from -0.1875 to 0.1875
- targets: int32 [768], replicated, may hold values from 0 to 65535
Outputs:
- head_grad: bfloat16 [2, 4096, 65536], P('copy', None, ('dp', 'vocab'))
- loss_mean: float32 [2], P('copy')
The draws below stay inside these ranges and needn't reach their ends.
All inputs are finite; a program needn't handle non-finite values.
Results may differ from the reference program's by a relative error of at most 0.0034.
Values may be sent and summed in bfloat16 or wider, within the bound.
A program may use at most 64 MiB of HBM per device.

```python
import math
import jax
import jax.numpy as jnp
import numpy as np

D = 4096
VOCAB = 65536
TOKENS = 768


def draw_hidden(key, part):
    value_key = jax.random.fold_in(jax.random.fold_in(key, 11), 0)
    values = jnp.clip(jax.random.normal(value_key, (2, TOKENS, D), jnp.float32), -6.0, 6.0)
    return values.astype(jnp.bfloat16)


def draw_head_weight(key, part):
    value_key = jax.random.fold_in(key, 23)
    spread = 3.0 / math.sqrt(D)
    values = jnp.clip(jax.random.normal(value_key, (2, D, VOCAB), jnp.float32), -4.0, 4.0) * spread
    return values.astype(jnp.bfloat16)


def set_ends(values, stream_key, low, top_value):
    longest = values.shape.index(max(values.shape))
    spots = []
    for shift in (0, 1):
        where = [jax.random.randint(jax.random.fold_in(stream_key, axis), (), 0, length) for axis, length in enumerate(values.shape)]
        where[longest] = (where[longest] + shift) % values.shape[longest]
        spots.append(tuple(where))
    return values.at[spots[0]].set(low).at[spots[1]].set(top_value)


def cumulative_ranks(number_of, skew):
    portions = [(1 << 20) // math.isqrt(grade ** skew) + 1 for grade in range(1, number_of + 1)]
    scale = 1 + sum(portions) // (1 << 30)
    return np.cumsum(np.array([max(1, weight // scale) for weight in portions]))


def ranked(stream_key, shape, amount, lean):
    table = cumulative_ranks(amount, lean)
    pick = jax.random.randint(jax.random.fold_in(stream_key, 1), shape, 0, int(table[amount - 1]))
    standing = jnp.searchsorted(jnp.asarray(table, jnp.int32), pick, side="right")
    return jax.random.permutation(jax.random.fold_in(stream_key, 2), amount)[standing].astype(jnp.int32)


def setup_inputs(seed: int = 0) -> dict:
    key_of = jax.random.split(jax.random.key(seed), 4)
    return {
        "hidden": draw_hidden(jax.random.fold_in(key_of[3], 71), 0),
        "head_weight": draw_head_weight(jax.random.fold_in(key_of[3], 71), 0),
        "targets": set_ends(ranked(key_of[2], (TOKENS,), VOCAB, 2), jax.random.fold_in(key_of[2], 3), 0, VOCAB - 1).astype(jnp.int32),
    }


distill_weight = 0.5


def reference(hidden, head_weight, targets):
    logit_pair = [jnp.dot(hidden[c], head_weight[c], preferred_element_type=jnp.float32) for c in range(2)]
    lse_pair = [jax.nn.logsumexp(logit_pair[c], axis=1) for c in range(2)]
    column_ids = jnp.arange(VOCAB, dtype=jnp.int32)
    onehot = (targets[:, None] == column_ids[None, :]).astype(jnp.float32)
    gradients = []
    loss_values = []
    for c in range(2):
        own_logits = logit_pair[c]
        other_logits = logit_pair[1 - c]
        own_probs = jnp.exp(own_logits - lse_pair[c][:, None])
        other_probs = jnp.exp(other_logits - lse_pair[1 - c][:, None])
        grad_logits = ((1.0 + distill_weight) * own_probs - onehot - distill_weight * other_probs).astype(jnp.bfloat16)
        gradients.append(jnp.dot(hidden[c].T, grad_logits, preferred_element_type=jnp.float32).astype(jnp.bfloat16))
        local_terms = jnp.sum(-onehot * own_logits + distill_weight * other_probs * (other_logits - own_logits))
        row_terms = jnp.sum((1.0 + distill_weight) * lse_pair[c] - distill_weight * lse_pair[1 - c])
        loss_values.append((row_terms + local_terms) / TOKENS)
    return jnp.stack(gradients), jnp.stack(loss_values)
```

```python
import functools

import jax
import jax.numpy as jnp
from jax import lax
from jax.experimental import pallas as pl
from jax.experimental.pallas import tpu as pltpu
from jax.sharding import Mesh
from jax.sharding import PartitionSpec as P

Z, Y, X, C = 16, 2, 4, 2
PEERS = Y * X * C
D = 4096
COLS = 256
ROWS = 3
PLANE = PEERS * ROWS
TOKENS = Z * PLANE
UNIT = D // PEERS
HALF = PEERS // 2
CHUNKS = 4
STEPS = Z // 2
LAG = 4
LANES = 128
GROUPS = TOKENS // LANES
TINY = 1e-37
DISTILL = 0.5

MESH = pl.DeviceIdType.MESH
F32 = jnp.float32
BF16 = jnp.bfloat16


def arrived(ref, sem):
    pltpu.make_async_copy(ref, ref, sem).wait()


def send(src, dst, send_sem, recv_sem, **where):
    pltpu.make_async_remote_copy(
        src_ref=src,
        dst_ref=dst,
        send_sem=send_sem,
        recv_sem=recv_sem,
        device_id=where,
        device_id_type=MESH,
    ).start()


def plane_peer(j):
    return {"y": j // (X * C), "x": lax.rem(j // C, X), "c": lax.rem(j, C)}


def kernel(
    hidden_ref, targets_ref, weight_hbm, grad_hbm, loss_ref,
    hbuf, weight, pad, abuf, logits, ebuf, pbuf, mcol, lcol,
    srow, s1, s2, prow, rrow, rbuf, lossv, lrow, l1, l2, obuf,
    wsem, osem, asem, zsem_a, zsem_b, bsem, ysem, xsem, qsem, csem, esem, ssem, rsem, out_sems,
):
    z, y, x, c = (lax.axis_index(n) for n in ("z", "y", "x", "c"))
    copy = lax.axis_index("copy")
    me = (y * X + x) * C + c
    unit = c * HALF + x * Y + y

    load_weight = pltpu.make_async_copy(weight_hbm, weight, wsem)
    load_weight.start()

    barrier = pltpu.get_barrier_semaphore()

    def greet(k, carry):
        pl.semaphore_signal(
            barrier, inc=1, device_id=plane_peer(lax.rem(me + k, PEERS)), device_id_type=MESH
        )
        pl.semaphore_signal(
            barrier, inc=1, device_id={"z": lax.rem(z + k, Z)}, device_id_type=MESH
        )
        return carry

    lax.fori_loop(1, PEERS, greet, 0)
    pl.semaphore_signal(barrier, inc=1, device_id={"copy": 1 - copy}, device_id_type=MESH)

    own = hidden_ref[0].astype(F32)
    pad[...] = jnp.zeros_like(pad)
    for q in range(PEERS):
        pad[q, 0:ROWS, :] = own[:, q * UNIT : (q + 1) * UNIT]

    pl.semaphore_wait(barrier, 2 * (PEERS - 1) + 1)

    def unit_of(j):
        return lax.rem(j, C) * HALF + lax.rem(j // C, X) * Y + j // (X * C)

    def scatter(k, carry):
        j = lax.rem(me + k, PEERS)
        send(pad.at[unit_of(j)], abuf.at[me], out_sems.at[0], asem, **plane_peer(j))
        return carry

    lax.fori_loop(1, PEERS, scatter, 0)
    abuf[pl.ds(me, 1)] = pad[pl.ds(unit, 1)]
    arrived(abuf.at[pl.ds(0, PEERS - 1)], asem)

    row = lax.broadcasted_iota(jnp.int32, (PLANE, PEERS * 8), 0)
    col = lax.broadcasted_iota(jnp.int32, (PLANE, PEERS * 8), 1)
    pick = (row == ROWS * (col >> 3) + (col & 7)) & ((col & 7) < ROWS)
    block = abuf[...].reshape(PEERS * 8, UNIT).astype(BF16)
    packed = jnp.dot(jnp.where(pick, 1.0, 0.0).astype(BF16), block, preferred_element_type=F32)
    hbuf[z, unit] = packed.astype(BF16)

    def at(p, first, count):
        return hbuf.at[p, pl.ds(first, count)]

    def back(t):
        return lax.rem(z - t + Z, Z)

    def ahead(t):
        return lax.rem(z + t, Z)

    right, left = ahead(1), back(1)

    def move(ref, sem_out, sem_in, **where):
        send(ref, ref, out_sems.at[sem_out], sem_in, **where)

    def a_enter(p, t, direction):
        ref = at(p, unit, 1)

        @pl.when(t > 0)
        def _():
            arrived(ref, zsem_a.at[direction, t])

        @pl.when(t < STEPS - direction)
        def _():
            move(ref, 1, zsem_a.at[direction, t + 1], z=right if direction == 0 else left)

    def a_first(p):
        move(at(p, unit, 1), 2, ysem.at[p], y=1 - y)

    def a_second(p):
        arrived(at(p, unit, 1), ysem.at[p])
        ref = at(p, x * Y, Y)
        move(ref, 3, xsem.at[0, p], x=lax.rem(x + 1, X))
        move(ref, 3, xsem.at[1, p], x=lax.rem(x + X - 1, X))
        move(ref, 4, csem.at[p], c=1 - c)

    def a_third(p):
        lower, upper = lax.rem(x + X - 1, X), lax.rem(x + 1, X)
        ref = at(p, lower * Y, Y)
        arrived(ref, xsem.at[0, p])
        move(at(p, lower * Y, 1), 5, qsem.at[p], x=upper)
        move(ref, 4, csem.at[p], c=1 - c)
        ref = at(p, upper * Y, Y)
        arrived(ref, xsem.at[1, p])
        move(at(p, upper * Y + 1, 1), 5, qsem.at[p], x=lower)
        move(ref, 4, csem.at[p], c=1 - c)

    def a_fourth(p):
        ref = at(p, lax.rem(x + 2, X) * Y, Y)
        arrived(ref, qsem.at[p])
        move(ref, 4, csem.at[p], c=1 - c)

    def for_planes(t, first, do):
        @pl.when((t >= first) & (t <= STEPS))
        def _():
            do(back(t))

        @pl.when((t >= 1) & (t <= STEPS - 1))
        def _():
            do(ahead(t))

    def b_spread(k, carry):
        j = lax.rem(me // C + k, HALF)
        move(at(z, unit, 1), 6, bsem, y=j // X, x=lax.rem(j, X))
        return carry

    def b_enter(p, t, direction):
        for k in range(CHUNKS):
            size = HALF // CHUNKS
            ref = at(p, HALF + k * size, size)

            @pl.when(t > 0)
            def _():
                arrived(ref, zsem_b.at[direction, t, k])

            @pl.when(t < STEPS - direction)
            def _():
                move(ref, 7, zsem_b.at[direction, t + 1, k], z=right if direction == 0 else left)

            if direction == 0:
                move(ref, 4, csem.at[p], c=1 - c)
            else:
                @pl.when(t > 0)
                def _():
                    move(ref, 4, csem.at[p], c=1 - c)

    @pl.when(c == 1)
    def _():
        lax.fori_loop(1, HALF, b_spread, 0)
        arrived(hbuf.at[z, pl.ds(HALF, HALF - 1)], bsem)

    load_weight.wait()

    def compute(u):
        planes = (back(u), ahead(u - 1))
        for p in planes:
            arrived(at(p, (1 - c) * HALF, HALF), csem.at[p])
        acc = jnp.zeros((2 * PLANE, COLS), F32)
        for q in range(PEERS):
            both = jnp.concatenate([hbuf[p, q] for p in planes], axis=0)
            acc += jnp.dot(both, weight[q * UNIT : (q + 1) * UNIT, :], preferred_element_type=F32)
        top = jnp.max(acc, axis=1, keepdims=True)
        e = jnp.exp(acc - top)
        lse = top + jnp.log(jnp.sum(e, axis=1, keepdims=True))
        for k, p in enumerate(planes):
            own_rows = slice(k * PLANE, (k + 1) * PLANE)
            rows = pl.ds(pl.multiple_of(p * PLANE, PLANE), PLANE)
            logits[rows, :] = acc[own_rows]
            mcol[rows, :] = top[own_rows]
            lcol[rows, :] = lse[own_rows]
            ebuf[rows, :] = e[own_rows].astype(BF16)
            send(
                ebuf.at[rows, :], pbuf.at[rows, :], out_sems.at[8], esem, copy=1 - copy
            )

    def step(i, carry):
        @pl.when(c == 0)
        def _():
            @pl.when(i <= STEPS)
            def _():
                a_enter(back(i), i, 0)

            @pl.when(i <= STEPS - 1)
            def _():
                a_enter(ahead(i), i, 1)

            for_planes(i, 0, a_first)
            for_planes(i - 1, 0, a_second)
            for_planes(i - 2, 0, a_third)
            for_planes(i - 3, 0, a_fourth)

        @pl.when(c == 1)
        def _():
            @pl.when(i <= STEPS)
            def _():
                b_enter(back(i), i, 0)

            @pl.when(i <= STEPS - 1)
            def _():
                b_enter(ahead(i), i, 1)

        @pl.when(i > LAG)
        def _():
            compute(i - LAG)

        return carry

    lax.fori_loop(0, STEPS + LAG + 1, step, 0)

    eye = lax.broadcasted_iota(jnp.int32, (LANES, LANES), 0) == lax.broadcasted_iota(
        jnp.int32, (LANES, LANES), 1
    )

    def to_row(column):
        return jnp.sum(jnp.where(eye, column, 0.0), axis=0, keepdims=True)

    def to_column(row):
        return jnp.sum(jnp.where(eye, row, 0.0), axis=1, keepdims=True)

    srow[...] = jnp.zeros_like(srow)
    for b in range(GROUPS):
        rows = slice(b * LANES, (b + 1) * LANES)
        srow[b : b + 1, :] = to_row(lcol[rows, :])

    def to_plane(src, dst, sem_out, sem_in):
        def one(k, carry):
            send(src, dst.at[me], out_sems.at[sem_out], sem_in, **plane_peer(lax.rem(me + k, PEERS)))
            return carry

        lax.fori_loop(1, PEERS, one, 0)
        dst[pl.ds(me, 1)] = src[...][None]

    def to_line(src, dst, sem_out, sem_in):
        def one(k, carry):
            send(src, dst.at[z], out_sems.at[sem_out], sem_in, z=lax.rem(z + k, Z))
            return carry

        lax.fori_loop(1, Z, one, 0)
        dst[pl.ds(z, 1)] = src[...][None]

    def merged(parts):
        top = jnp.max(parts, axis=0)
        return top + jnp.log(jnp.sum(jnp.exp(parts - top[None]), axis=0))

    to_plane(srow, s1, 9, ssem.at[0])
    arrived(s1.at[pl.ds(0, PEERS - 1)], ssem.at[0])
    prow[...] = merged(s1[...])
    to_line(prow, s2, 10, ssem.at[1])
    arrived(s2.at[pl.ds(0, Z - 1)], ssem.at[1])
    total = merged(s2[...])

    rrow[...] = jnp.zeros_like(rrow)
    for b in range(GROUPS):
        rows = slice(b * LANES, (b + 1) * LANES)
        rrow[b : b + 1, :] = to_row(mcol[rows, :]) - total[b : b + 1, :]
    send(rrow, rbuf, out_sems.at[11], rsem, copy=1 - copy)
    arrived(rbuf, rsem)
    arrived(pbuf, esem)

    offset = ((z * Y + y) * (X * C) + x * C + c) * COLS
    ids = offset + lax.broadcasted_iota(jnp.int32, (LANES, COLS), 1)
    loss = jnp.zeros((8, COLS), F32)
    grads = []
    for b in range(GROUPS):
        rows = slice(b * LANES, (b + 1) * LANES)
        log_p = logits[rows, :] - to_column(total[b : b + 1, :])
        log_scale = to_column(rbuf[b : b + 1, :])
        other = pbuf[rows, :].astype(F32)
        log_o = jnp.log(jnp.maximum(other, TINY)) + log_scale
        other = other * jnp.exp(log_scale)
        target = to_column(targets_ref[b : b + 1, :].astype(F32)).astype(jnp.int32)
        hot = jnp.where(ids == target, 1.0, 0.0)
        grads.append(((1.0 + DISTILL) * jnp.exp(log_p) - hot - DISTILL * other).astype(BF16).T)
        terms = DISTILL * other * (log_o - log_p) - hot * log_p
        loss += jnp.sum(terms.reshape(LANES // 8, 8, COLS), axis=0)
    grads = jnp.concatenate(grads, axis=1)
    lossv[...] = loss[:, :LANES] + loss[:, LANES:]
    to_plane(lossv, l1, 12, ssem.at[2])

    def grad_piece(q):
        block = hbuf[:, q].reshape(TOKENS, UNIT)
        flipped = jnp.dot(grads, block, preferred_element_type=F32)
        obuf[q] = flipped.astype(BF16).T
        pltpu.make_async_copy(obuf.at[q], grad_hbm.at[pl.ds(q * UNIT, UNIT), :], osem).start()

    for q in range(HALF):
        grad_piece(q)
    arrived(l1.at[pl.ds(0, PEERS - 1)], ssem.at[2])
    lrow[...] = jnp.sum(l1[...], axis=0)
    for q in range(HALF, PEERS):
        grad_piece(q)
    to_line(lrow, l2, 13, ssem.at[3])
    arrived(l2.at[pl.ds(0, Z - 1)], ssem.at[3])
    loss_ref[0] = jnp.sum(l2[...]) * (1.0 / TOKENS)

    units = hbuf.at[0]
    arrived(pad.at[pl.ds(0, PEERS - 1)], out_sems.at[0])
    arrived(hbuf.at[pl.ds(0, HALF)], out_sems.at[4])

    @pl.when(c == 0)
    def _():
        arrived(units.at[pl.ds(0, Z - 1)], out_sems.at[1])
        arrived(units, out_sems.at[2])
        arrived(hbuf.at[pl.ds(0, 4)], out_sems.at[3])
        arrived(hbuf.at[pl.ds(0, 2)], out_sems.at[5])

    @pl.when(c == 1)
    def _():
        arrived(units.at[pl.ds(0, HALF - 1)], out_sems.at[6])
        arrived(hbuf.at[pl.ds(0, Z - 1), pl.ds(0, HALF)], out_sems.at[7])

    arrived(ebuf, out_sems.at[8])
    arrived(s1.at[pl.ds(0, PEERS - 1)], out_sems.at[9])
    arrived(s1.at[pl.ds(0, Z - 1)], out_sems.at[10])
    arrived(rrow, out_sems.at[11])
    arrived(s1.at[pl.ds(0, PEERS - 1)], out_sems.at[12])
    arrived(s1.at[pl.ds(0, Z - 1)], out_sems.at[13])
    arrived(obuf, osem)


def body(hidden, head_weight, targets):
    dma = pltpu.SemaphoreType.DMA
    stat = (8, LANES)
    grad, loss = pl.pallas_call(
        kernel,
        out_shape=(
            jax.ShapeDtypeStruct((D, COLS), BF16),
            jax.ShapeDtypeStruct((1,), F32),
        ),
        in_specs=[
            pl.BlockSpec(memory_space=pltpu.VMEM),
            pl.BlockSpec(memory_space=pltpu.VMEM),
            pl.BlockSpec(memory_space=pl.ANY),
        ],
        out_specs=(
            pl.BlockSpec(memory_space=pl.ANY),
            pl.BlockSpec(memory_space=pltpu.SMEM),
        ),
        scratch_shapes=[
            pltpu.VMEM((Z, PEERS, PLANE, UNIT), BF16),
            pltpu.VMEM((D, COLS), BF16),
            pltpu.VMEM((PEERS, 8, UNIT), F32),
            pltpu.VMEM((PEERS, 8, UNIT), F32),
            pltpu.VMEM((TOKENS, COLS), F32),
            pltpu.VMEM((TOKENS, COLS), BF16),
            pltpu.VMEM((TOKENS, COLS), BF16),
            pltpu.VMEM((TOKENS, 1), F32),
            pltpu.VMEM((TOKENS, 1), F32),
            pltpu.VMEM(stat, F32),
            pltpu.VMEM((PEERS, *stat), F32),
            pltpu.VMEM((Z, *stat), F32),
            pltpu.VMEM(stat, F32),
            pltpu.VMEM(stat, F32),
            pltpu.VMEM(stat, F32),
            pltpu.VMEM(stat, F32),
            pltpu.VMEM(stat, F32),
            pltpu.VMEM((PEERS, *stat), F32),
            pltpu.VMEM((Z, *stat), F32),
            pltpu.VMEM((PEERS, UNIT, COLS), BF16),
            dma,
            dma,
            dma,
            dma((2, STEPS + 1)),
            dma((2, STEPS + 1, CHUNKS)),
            dma,
            dma((Z,)),
            dma((2, Z)),
            dma((Z,)),
            dma((Z,)),
            dma,
            dma((4,)),
            dma,
            dma((14,)),
        ],
        compiler_params=pltpu.CompilerParams(
            collective_id=0, has_side_effects=True, vmem_limit_bytes=48 * 1024 * 1024
        ),
        cost_estimate=pl.CostEstimate(
            flops=4 * TOKENS * D * COLS,
            bytes_accessed=4 * D * COLS,
            transcendentals=3 * TOKENS * COLS,
        ),
    )(hidden, targets.reshape(GROUPS, LANES), head_weight[0])
    return grad[None], loss


def solution(mesh):
    torus = Mesh(
        mesh.devices.reshape(mesh.shape["copy"], Z, Y, X, C), ("copy", "z", "y", "x", "c")
    )
    everywhere = ("z", "y", "x", "c")
    in_specs = (P("copy", everywhere, None), P("copy", None, everywhere), P())
    out_specs = (P("copy", None, everywhere), P("copy"))
    return jax.shard_map(body, mesh=torus, in_specs=in_specs, out_specs=out_specs, check_vma=False)
```

```python
import jax
import jax.numpy as jnp
from jax import lax
from jax.experimental import pallas as pl
from jax.experimental.pallas import tpu as pltpu
from jax.sharding import Mesh
from jax.sharding import PartitionSpec as P

Z, Y, X, C = 16, 2, 4, 2
PEERS = Y * X * C
D = 4096
COLS = 256
ROWS = 3
PLANE = PEERS * ROWS
TOKENS = Z * PLANE
UNIT = D // PEERS
HALF = PEERS // 2
CHUNKS = 4
STEPS = Z // 2
LAG = 3
LANES = 128
GROUPS = TOKENS // LANES
TINY = 1e-37
DISTILL = 0.5
VMEM_BYTES = 63 * 1024 * 1024

MESH = pl.DeviceIdType.MESH
F32 = jnp.float32
BF16 = jnp.bfloat16


def arrived(ref, sem):
    pltpu.make_async_copy(ref, ref, sem).wait()


def send(src, dst, send_sem, recv_sem, **where):
    pltpu.make_async_remote_copy(
        src_ref=src,
        dst_ref=dst,
        send_sem=send_sem,
        recv_sem=recv_sem,
        device_id=where,
        device_id_type=MESH,
    ).start()


def plane_peer(j):
    return {"y": j // (X * C), "x": lax.rem(j // C, X), "c": lax.rem(j, C)}


def kernel(
    hidden_hbm, targets_hbm, weight_hbm, grad_hbm, loss_ref,
    own_rows, targets, weight, hbuf, pad, abuf, logits, ebuf, pbuf, gt, tcol, mcol, lcol, tsum,
    lrow, mrow, plrow, pmrow, s1, prow, s2, trow, ptrow, kmsg, k1, zmsg, z1, obuf,
    wsem, hsem, tsem, asem, zsem_a, zsem_b, bsem, ysem, xsem, csem, esem, ssem, osem, out_sems,
):
    z, y, x, c = (lax.axis_index(n) for n in ("z", "y", "x", "c"))
    copy = lax.axis_index("copy")
    me = (y * X + x) * C + c
    unit = c * HALF + x * Y + y

    load_rows = pltpu.make_async_copy(hidden_hbm.at[0], own_rows, hsem)
    load_rows.start()

    def back(t):
        return lax.rem(z - t + Z, Z)

    def ahead(t):
        return lax.rem(z + t, Z)

    right, left = ahead(1), back(1)
    barrier = pltpu.get_barrier_semaphore()

    def meet(**where):
        pl.semaphore_signal(barrier, inc=1, device_id=where, device_id_type=MESH)

    def greet(k, carry):
        meet(**plane_peer(lax.rem(me + k, PEERS)))
        return carry

    meet(z=right)
    meet(z=left)
    meet(copy=1 - copy)
    lax.fori_loop(1, PEERS, greet, 0)

    load_targets = pltpu.make_async_copy(targets_hbm, targets, tsem)
    load_targets.start()
    load_weight = pltpu.make_async_copy(weight_hbm, weight, wsem)
    load_weight.start()

    pad[...] = jnp.zeros_like(pad)
    load_rows.wait()
    own = own_rows[...].astype(F32)
    for q in range(PEERS):
        pad[q, 0:ROWS, :] = own[:, q * UNIT : (q + 1) * UNIT]

    pl.semaphore_wait(barrier, PEERS + 2)

    def unit_of(j):
        return lax.rem(j, C) * HALF + lax.rem(j // C, X) * Y + j // (X * C)

    def scatter(k, carry):
        j = lax.rem(me + k, PEERS)
        send(pad.at[unit_of(j)], abuf.at[me], out_sems.at[0], asem, **plane_peer(j))
        return carry

    lax.fori_loop(1, PEERS, scatter, 0)
    abuf[pl.ds(me, 1)] = pad[pl.ds(unit, 1)]

    row = lax.broadcasted_iota(jnp.int32, (PLANE, PEERS * 8), 0)
    col = lax.broadcasted_iota(jnp.int32, (PLANE, PEERS * 8), 1)
    pick = (row == ROWS * (col >> 3) + (col & 7)) & ((col & 7) < ROWS)
    pick = jnp.where(pick, 1.0, 0.0).astype(BF16)

    eye = lax.broadcasted_iota(jnp.int32, (LANES, LANES), 0) == lax.broadcasted_iota(
        jnp.int32, (LANES, LANES), 1
    )

    def to_row(column):
        return jnp.sum(jnp.where(eye, column, 0.0), axis=0, keepdims=True)

    def to_column(row):
        return jnp.sum(jnp.where(eye, row, 0.0), axis=1, keepdims=True)

    def group(b):
        return slice(b * LANES, (b + 1) * LANES)

    load_targets.wait()
    for b in range(GROUPS):
        tcol[group(b), :] = to_column(targets[b : b + 1, :].astype(F32)).astype(jnp.int32)
    tsum[...] = jnp.zeros_like(tsum)
    offset = ((z * Y + y) * (X * C) + x * C + c) * COLS

    arrived(abuf.at[pl.ds(0, PEERS - 1)], asem)
    block = abuf[...].reshape(PEERS * 8, UNIT).astype(BF16)
    hbuf[z, unit] = jnp.dot(pick, block, preferred_element_type=F32).astype(BF16)

    def at(p, first, count):
        return hbuf.at[p, pl.ds(first, count)]

    def move(ref, sem_out, sem_in, **where):
        send(ref, ref, out_sems.at[sem_out], sem_in, **where)

    def onward(direction):
        return right if direction == 0 else left

    def for_planes(t, do):
        @pl.when((t >= 0) & (t <= STEPS))
        def _():
            do(back(t))

        @pl.when((t >= 1) & (t <= STEPS - 1))
        def _():
            do(ahead(t))

    def a_enter(p, t, direction):
        ref = at(p, unit, 1)

        @pl.when(t > 0)
        def _():
            arrived(ref, zsem_a.at[direction, t])

        @pl.when(t < STEPS - direction)
        def _():
            move(ref, 1, zsem_a.at[direction, t + 1], z=onward(direction))

    def a_first(p):
        move(at(p, unit, 1), 2, ysem.at[p], y=1 - y)

    def a_second(p):
        arrived(at(p, unit, 1), ysem.at[p])
        ref = at(p, x * Y, Y)
        for k in range(1, X):
            move(ref, 3, xsem.at[k - 1, p], x=lax.rem(x + k, X))

    def a_third(p):
        for k in range(1, X):
            arrived(at(p, lax.rem(x + X - k, X) * Y, Y), xsem.at[k - 1, p])
        move(at(p, 0, HALF), 4, csem.at[p], c=1 - c)

    def a_step(i):
        @pl.when(i <= STEPS)
        def _():
            a_enter(back(i), i, 0)

        @pl.when(i <= STEPS - 1)
        def _():
            a_enter(ahead(i), i, 1)

        for_planes(i, a_first)
        for_planes(i - 1, a_second)
        for_planes(i - 2, a_third)

    def b_spread(k, carry):
        j = lax.rem(me // C + k, HALF)
        move(at(z, unit, 1), 5, bsem, y=j // X, x=lax.rem(j, X))
        return carry

    def b_enter(p, t, direction, k):
        size = HALF // CHUNKS
        ref = at(p, HALF + k * size, size)

        @pl.when(t > 0)
        def _():
            arrived(ref, zsem_b.at[direction, t, k])

        @pl.when(t < STEPS - direction)
        def _():
            move(ref, 6, zsem_b.at[direction, t + 1, k], z=onward(direction))

    def b_share(p):
        move(at(p, HALF, HALF), 4, csem.at[p], c=1 - c)

    def b_step(i):
        for k in range(CHUNKS):
            @pl.when(i <= STEPS)
            def _():
                b_enter(back(i), i, 0, k)

            @pl.when(i <= STEPS - 1)
            def _():
                b_enter(ahead(i), i, 1, k)

        for_planes(i, b_share)

    @pl.when(c == 1)
    def _():
        lax.fori_loop(1, HALF, b_spread, 0)
        arrived(hbuf.at[z, pl.ds(HALF, HALF - 1)], bsem)

    load_weight.wait()

    def compute(u):
        planes = (back(u), ahead(u - 1))
        for p in planes:
            arrived(at(p, (1 - c) * HALF, HALF), csem.at[p])
        acc = jnp.zeros((2 * PLANE, COLS), F32)
        for q in range(PEERS):
            both = jnp.concatenate([hbuf[p, q] for p in planes], axis=0)
            acc += jnp.dot(both, weight[q * UNIT : (q + 1) * UNIT, :], preferred_element_type=F32)
        top = jnp.max(acc, axis=1, keepdims=True)
        e = jnp.exp(acc - top)
        lse = top + jnp.log(jnp.sum(e, axis=1, keepdims=True))
        ids = offset + lax.broadcasted_iota(jnp.int32, (PLANE, COLS), 1)
        for k, p in enumerate(planes):
            mine = slice(k * PLANE, (k + 1) * PLANE)
            rows = pl.ds(pl.multiple_of(p * PLANE, PLANE), PLANE)
            logits[rows, :] = acc[mine]
            mcol[rows, :] = top[mine]
            lcol[rows, :] = lse[mine]
            ebuf[rows, :] = e[mine].astype(BF16)
            send(ebuf.at[rows, :], pbuf.at[rows, :], out_sems.at[7], esem, copy=1 - copy)
            hit = jnp.where(ids == tcol[rows, :], acc[mine], 0.0)
            tsum[...] += jnp.sum(hit.reshape(PLANE // 8, 8, COLS), axis=0)

    def step(i, carry):
        @pl.when(c == 0)
        def _():
            a_step(i)

        @pl.when(c == 1)
        def _():
            b_step(i)

        @pl.when(i > LAG)
        def _():
            compute(i - LAG)

        return carry

    lax.fori_loop(0, STEPS + LAG + 1, step, 0)

    def to_plane(src, dst, sem_out, sem_in):
        def one(k, carry):
            send(src, dst.at[me], out_sems.at[sem_out], sem_in, **plane_peer(lax.rem(me + k, PEERS)))
            return carry

        lax.fori_loop(1, PEERS, one, 0)
        dst[pl.ds(me, 1)] = src[...][None]

    def to_line(src, dst, sem_out, sem_in):
        def one(k, carry):
            send(src, dst.at[z], out_sems.at[sem_out], sem_in, z=lax.rem(z + k, Z))
            return carry

        lax.fori_loop(1, Z, one, 0)
        dst[pl.ds(z, 1)] = src[...][None]

    def merged(parts):
        top = jnp.max(parts, axis=0)
        return top + jnp.log(jnp.sum(jnp.exp(parts - top[None]), axis=0))

    for b in range(GROUPS):
        lrow[b : b + 1, :] = to_row(lcol[group(b), :])
    to_plane(lrow, s1, 8, ssem.at[0])
    send(lrow, plrow, out_sems.at[9], ssem.at[1], copy=1 - copy)
    for b in range(GROUPS):
        mrow[b : b + 1, :] = to_row(mcol[group(b), :])
    send(mrow, pmrow, out_sems.at[10], ssem.at[2], copy=1 - copy)
    arrived(s1.at[pl.ds(0, PEERS - 1)], ssem.at[0])
    prow[...] = merged(s1[...])
    to_line(prow, s2, 11, ssem.at[3])

    arrived(plrow, ssem.at[1])
    arrived(pmrow, ssem.at[2])
    arrived(pbuf, esem)
    kmsg[...] = jnp.zeros_like(kmsg)
    for b in range(GROUPS):
        other = pbuf[group(b), :].astype(F32)
        apart = jnp.log(jnp.maximum(other, TINY)) - logits[group(b), :]
        weighted = jnp.sum(other * apart, axis=1, keepdims=True)
        mean = to_row(weighted / jnp.sum(other, axis=1, keepdims=True))
        kmsg[b : b + 1, :] = mean + pmrow[b : b + 1, :]
        kmsg[8 + b : 9 + b, :] = plrow[b : b + 1, :]
    hits = jnp.sum(tsum[...], axis=0, keepdims=True)
    kmsg[GROUPS : GROUPS + 1, :] = hits[:, :LANES] + hits[:, LANES:]
    to_plane(kmsg, k1, 12, ssem.at[4])

    arrived(s2.at[pl.ds(0, Z - 1)], ssem.at[3])
    trow[...] = merged(s2[...])
    send(trow, ptrow, out_sems.at[13], ssem.at[5], copy=1 - copy)

    total = trow[...]
    ids = offset + lax.broadcasted_iota(jnp.int32, (LANES, COLS), 1)
    for b in range(GROUPS):
        probs = jnp.exp(logits[group(b), :] - to_column(total[b : b + 1, :]))
        hot = jnp.where(ids == tcol[group(b), :], 1.0, 0.0)
        logits[group(b), :] = (1.0 + DISTILL) * probs - hot
    arrived(k1.at[pl.ds(0, PEERS - 1)], ssem.at[4])
    plane_kl = k1[:, 0:GROUPS, :]
    plane_lse = k1[:, 8 : 8 + GROUPS, :]
    plane_hits = jnp.sum(k1[:, GROUPS : GROUPS + 1, :], axis=0)

    arrived(ptrow, ssem.at[5])
    partner_total = ptrow[...]
    kl = jnp.sum(jnp.exp(plane_lse - partner_total[None]) * plane_kl, axis=0)
    zmsg[...] = DISTILL * jnp.sum(kl, axis=0, keepdims=True) - plane_hits
    to_line(zmsg, z1, 14, ssem.at[6])

    scale = DISTILL * jnp.exp(pmrow[...] - partner_total)
    for b in range(GROUPS):
        other = pbuf[group(b), :].astype(F32) * to_column(scale[b : b + 1, :])
        gt[:, group(b)] = (logits[group(b), :] - other).astype(BF16).T

    for q in range(PEERS):
        block = hbuf[:, q].reshape(TOKENS, UNIT)
        flipped = jnp.dot(gt[...], block, preferred_element_type=F32)
        obuf[q] = flipped.astype(BF16).T
        pltpu.make_async_copy(obuf.at[q], grad_hbm.at[pl.ds(q * UNIT, UNIT), :], osem).start()

    arrived(z1.at[pl.ds(0, Z - 1)], ssem.at[6])
    per_token = (1.0 + DISTILL) * total - DISTILL * partner_total
    loss_ref[0] = (jnp.sum(z1[...]) + jnp.sum(per_token)) * (1.0 / TOKENS)

    units = hbuf.at[0]
    arrived(pad.at[pl.ds(0, PEERS - 1)], out_sems.at[0])
    arrived(hbuf.at[pl.ds(0, HALF)], out_sems.at[4])

    @pl.when(c == 0)
    def _():
        arrived(units.at[pl.ds(0, Z - 1)], out_sems.at[1])
        arrived(units, out_sems.at[2])
        arrived(hbuf.at[pl.ds(0, 2 * (X - 1))], out_sems.at[3])

    @pl.when(c == 1)
    def _():
        arrived(units.at[pl.ds(0, HALF - 1)], out_sems.at[5])
        arrived(hbuf.at[pl.ds(0, Z - 1), pl.ds(0, HALF)], out_sems.at[6])

    arrived(ebuf, out_sems.at[7])
    arrived(s1.at[pl.ds(0, PEERS - 1)], out_sems.at[8])
    arrived(lrow, out_sems.at[9])
    arrived(mrow, out_sems.at[10])
    arrived(s2.at[pl.ds(0, Z - 1)], out_sems.at[11])
    arrived(k1.at[pl.ds(0, PEERS - 1)], out_sems.at[12])
    arrived(trow, out_sems.at[13])
    arrived(z1.at[pl.ds(0, Z - 1)], out_sems.at[14])
    arrived(obuf, osem)


def body(hidden, head_weight, targets):
    dma = pltpu.SemaphoreType.DMA
    stat = pltpu.VMEM((GROUPS, LANES), F32)
    hbm = pl.BlockSpec(memory_space=pltpu.HBM)
    grad, loss = pl.pallas_call(
        kernel,
        out_shape=(
            jax.ShapeDtypeStruct((D, COLS), BF16),
            jax.ShapeDtypeStruct((1,), F32),
        ),
        in_specs=[hbm, hbm, hbm],
        out_specs=(
            hbm,
            pl.BlockSpec(memory_space=pltpu.SMEM),
        ),
        scratch_shapes=[
            pltpu.VMEM((ROWS, D), BF16),
            pltpu.VMEM((GROUPS, LANES), jnp.int32),
            pltpu.VMEM((D, COLS), BF16),
            pltpu.VMEM((Z, PEERS, PLANE, UNIT), BF16),
            pltpu.VMEM((PEERS, 8, UNIT), F32),
            pltpu.VMEM((PEERS, 8, UNIT), F32),
            pltpu.VMEM((TOKENS, COLS), F32),
            pltpu.VMEM((TOKENS, COLS), BF16),
            pltpu.VMEM((TOKENS, COLS), BF16),
            pltpu.VMEM((COLS, TOKENS), BF16),
            pltpu.VMEM((TOKENS, 1), jnp.int32),
            pltpu.VMEM((TOKENS, 1), F32),
            pltpu.VMEM((TOKENS, 1), F32),
            pltpu.VMEM((8, COLS), F32),
            stat,
            stat,
            stat,
            stat,
            pltpu.VMEM((PEERS, GROUPS, LANES), F32),
            stat,
            pltpu.VMEM((Z, GROUPS, LANES), F32),
            stat,
            stat,
            pltpu.VMEM((16, LANES), F32),
            pltpu.VMEM((PEERS, 16, LANES), F32),
            pltpu.VMEM((1, LANES), F32),
            pltpu.VMEM((Z, 1, LANES), F32),
            pltpu.VMEM((PEERS, UNIT, COLS), BF16),
            dma,
            dma,
            dma,
            dma,
            dma((2, STEPS + 1)),
            dma((2, STEPS + 1, CHUNKS)),
            dma,
            dma((Z,)),
            dma((X - 1, Z)),
            dma((Z,)),
            dma,
            dma((7,)),
            dma,
            dma((15,)),
        ],
        compiler_params=pltpu.CompilerParams(
            collective_id=0, has_side_effects=True, vmem_limit_bytes=VMEM_BYTES
        ),
        cost_estimate=pl.CostEstimate(
            flops=4 * TOKENS * D * COLS,
            bytes_accessed=4 * D * COLS,
            transcendentals=3 * TOKENS * COLS,
        ),
    )(hidden, targets.reshape(GROUPS, LANES), head_weight[0])
    return grad[None], loss


def solution(mesh):
    torus = Mesh(
        mesh.devices.reshape(mesh.shape["copy"], Z, Y, X, C), ("copy", "z", "y", "x", "c")
    )
    everywhere = ("z", "y", "x", "c")
    in_specs = (P("copy", everywhere, None), P("copy", None, everywhere), P())
    out_specs = (P("copy", None, everywhere), P("copy"))
    return jax.shard_map(body, mesh=torus, in_specs=in_specs, out_specs=out_specs, check_vma=False)
```

```python
import jax
import jax.numpy as jnp
from jax import lax
from jax.experimental import pallas as pl
from jax.experimental.pallas import tpu as pltpu
from jax.sharding import Mesh
from jax.sharding import PartitionSpec as P

Z, Y, X, C = 16, 2, 4, 2
PEERS = Y * X * C
D = 4096
COLS = 256
ROWS = 3
PLANE = PEERS * ROWS
TOKENS = Z * PLANE
CHIPS = X * Y
UNIT = 256
SPLIT = CHIPS * UNIT
SUBS = 2 * CHIPS
CHUNKS = 4
STEPS = Z // 2
LAG = 4
LANES = 128
GROUPS = TOKENS // LANES
TINY = 1e-37
DISTILL = 0.5
VMEM_BYTES = 63 * 1024 * 1024

ARRIVE = ((0, 1), (15, 2), (4, 12), (8, 3), (13, 5), (11, 14), (6, 10), (7, 9))
WORK = ((0, 1), (15, 2), (4, 12), (3, 13), (5, 11), (14, 6), (10, 7), (9, 8))

MESH = pl.DeviceIdType.MESH
F32 = jnp.float32
BF16 = jnp.bfloat16


def arrived(ref, sem):
    pltpu.make_async_copy(ref, ref, sem).wait()


def send(src, dst, send_sem, recv_sem, **where):
    pltpu.make_async_remote_copy(
        src_ref=src,
        dst_ref=dst,
        send_sem=send_sem,
        recv_sem=recv_sem,
        device_id=where,
        device_id_type=MESH,
    ).start()


def plane_peer(j):
    return {"y": j // (X * C), "x": lax.rem(j // C, X), "c": lax.rem(j, C)}


def kernel(
    hidden_hbm, targets_hbm, weight_hbm, grad_hbm, loss_ref,
    own_rows, targets, weight, ha, hb, stage_a, stage_b, pad_a, pad_b, abuf_a, abuf_b, logits, ebuf, pbuf, gt, tcol, mcol, lcol, tsum,
    lrow, mrow, plrow, pmrow, s1, prow, s2, trow, ptrow, kmsg, k1, krow, zmsg, z1, lossv, l1, obuf,
    wsem, hsem, tsem, asem, zsem_a, zsem_b, ysem, xsem, csem, esem, ssem, osem, near, out_sems,
):
    z, y, x, c = (lax.axis_index(n) for n in ("z", "y", "x", "c"))
    copy = lax.axis_index("copy")
    me = (y * X + x) * C + c
    unit = x * Y + y

    load_rows = pltpu.make_async_copy(hidden_hbm.at[0], own_rows, hsem)
    load_rows.start()

    def back(t):
        return lax.rem(z - t + Z, Z)

    def ahead(t):
        return lax.rem(z + t, Z)

    right, left = ahead(1), back(1)
    barrier = pltpu.get_barrier_semaphore()

    def meet(**where):
        pl.semaphore_signal(barrier, inc=1, device_id=where, device_id_type=MESH)

    def greet(k, carry):
        meet(**plane_peer(lax.rem(me + k, PEERS)))
        return carry

    meet(z=right)
    meet(z=left)
    meet(copy=1 - copy)
    lax.fori_loop(1, PEERS, greet, 0)

    load_targets = pltpu.make_async_copy(targets_hbm, targets, tsem)
    load_targets.start()
    load_weight = pltpu.make_async_copy(weight_hbm, weight, wsem)
    load_weight.start()

    stage_a[...] = jnp.zeros_like(stage_a)
    load_rows.wait()
    own = own_rows[...].astype(F32)
    for s in range(SUBS):
        for r in range(ROWS):
            half = own[r : r + 1, s * LANES : (s + 1) * LANES]
            stage_a[s // 2, 2 * r + s % 2 : 2 * r + s % 2 + 1, :] = half
            half = own[r : r + 1, SPLIT + s * LANES : SPLIT + (s + 1) * LANES]
            stage_b[s : s + 1, r * LANES : (r + 1) * LANES] = half
    pad_a[...] = stage_a[...].astype(BF16)
    pad_b[...] = stage_b[...].astype(BF16)

    pl.semaphore_wait(barrier, PEERS + 2)

    def give_first(y_to, x_to):
        send(
            pad_a.at[x_to * Y + y_to], abuf_a.at[me], out_sems.at[0], asem, y=y_to, x=x_to, c=0
        )

    def give_last(y_to, x_to):
        send(pad_b, abuf_b.at[me], out_sems.at[15], asem, y=y_to, x=x_to, c=1)

    def scatter(k, carry):
        chip = lax.rem(me // C + k, CHIPS)
        give_last(chip // X, lax.rem(chip, X))
        give_first(chip // X, lax.rem(chip, X))
        return carry

    lax.fori_loop(1, CHIPS, scatter, 0)

    @pl.when(c == 0)
    def _():
        give_last(y, x)
        abuf_a[pl.ds(me, 1)] = pad_a[pl.ds(unit, 1)]

    @pl.when(c == 1)
    def _():
        give_first(y, x)
        abuf_b[pl.ds(me, 1)] = pad_b[...][None]

    eye = lax.broadcasted_iota(jnp.int32, (LANES, LANES), 0) == lax.broadcasted_iota(
        jnp.int32, (LANES, LANES), 1
    )

    def to_row(column):
        return jnp.sum(jnp.where(eye, column, 0.0), axis=0, keepdims=True)

    def to_column(row):
        return jnp.sum(jnp.where(eye, row, 0.0), axis=1, keepdims=True)

    def group(b):
        return slice(b * LANES, (b + 1) * LANES)

    def selector(height, source):
        row = lax.broadcasted_iota(jnp.int32, (height, PEERS * 16), 0)
        col = lax.broadcasted_iota(jnp.int32, (1, PEERS * 16), 1)
        return jnp.where(row == source(col >> 4, col & 15), 1.0, 0.0).astype(BF16)

    def pick(chosen, block):
        return jnp.dot(chosen, block, preferred_element_type=F32)

    def move(ref, sem_out, sem_in, **where):
        send(ref, ref, out_sems.at[sem_out], sem_in, **where)

    def entry(table, t, k):
        digits = sum(pair[k] << (4 * n) for n, pair in enumerate(table[:7]))
        return jnp.where(t == 7, table[7][k], (digits >> (4 * jnp.minimum(t, 6))) & 15)

    def a_onward(p):
        for to in (right, left, ahead(2)):
            move(ha.at[p, unit], 1, zsem_a.at[p], z=to)

    def a_enter(p, further, opposite=False):
        ref = ha.at[p, unit]

        @pl.when(p != z)
        def _():
            arrived(ref, zsem_a.at[p])

        @pl.when(further)
        def _():
            a_onward(p)

        @pl.when(opposite)
        def _():
            move(ref, 1, zsem_a.at[p], z=ahead(4))

        move(ref, 2, ysem.at[p], y=1 - y)

    def a_second(p):
        arrived(ha.at[p, unit], ysem.at[p])
        ref = ha.at[p, pl.ds(x * Y, Y)]
        for k in range(1, X):
            move(ref, 3, xsem.at[k - 1, p], x=lax.rem(x + k, X))

    def a_third(p):
        for k in range(1, X):
            arrived(ha.at[p, pl.ds(lax.rem(x + X - k, X) * Y, Y)], xsem.at[k - 1, p])
        move(ha.at[p], 4, csem.at[p], c=1 - c)

    def a_step(i):
        @pl.when(i < STEPS)
        def _():
            a_enter(back(entry(ARRIVE, i, 0)), (i == 2) | (i == 3), i == 2)
            a_enter(back(entry(ARRIVE, i, 1)), i == 2)

        for lag, do in ((1, a_second), (3, a_third)):
            @pl.when((i >= lag) & (i < STEPS + lag))
            def _():
                for k in range(2):
                    do(back(entry(ARRIVE, i - lag, k)))

    @pl.when(c == 0)
    def _():
        for distance in (1, 2):
            for p in (ahead(distance), back(distance)):
                pl.semaphore_signal(
                    near.at[distance - 1], inc=1, device_id={"z": p}, device_id_type=MESH
                )
            pl.semaphore_wait(near.at[distance - 1], 2)
        chosen = []
        for h in range(2):
            def source(j, at, h=h):
                used = (at < 2 * ROWS) & ((at & 1) == h)
                return jnp.where(used, ROWS * j + (at >> 1), -1)

            chosen.append(selector(PLANE, source))
        arrived(abuf_a.at[pl.ds(0, PEERS - 1)], asem)
        block = abuf_a[...].reshape(PEERS * 16, LANES)
        halves = [pick(one, block) for one in chosen]
        ha[z, unit] = jnp.concatenate(halves, axis=1).astype(BF16)
        for p in (ahead(4), back(4)):
            move(ha.at[z, unit], 1, zsem_a.at[z], z=p)
        a_onward(z)

    def b_enter(p, t, direction, k):
        size = CHIPS // CHUNKS
        ref = hb.at[p, pl.ds(k * size, size)]

        @pl.when(t > 0)
        def _():
            arrived(ref, zsem_b.at[direction, t, k])

        @pl.when(t < STEPS - direction)
        def _():
            move(ref, 6, zsem_b.at[direction, t + 1, k], z=right if direction == 0 else left)

    def b_share(p):
        move(hb.at[p], 5, csem.at[p], c=1 - c)

    def b_step(i):
        for k in range(CHUNKS):
            @pl.when(i <= STEPS)
            def _():
                b_enter(back(i), i, 0, k)

            @pl.when(i < STEPS)
            def _():
                b_enter(ahead(i), i, 1, k)

        @pl.when(i <= STEPS)
        def _():
            b_share(back(i))

        @pl.when((i >= 1) & (i < STEPS))
        def _():
            b_share(ahead(i))

    @pl.when(c == 1)
    def _():
        chosen = [
            selector(SUBS * PLANE, lambda j, s, r=r: s * PLANE + ROWS * j + r) for r in range(ROWS)
        ]
        arrived(abuf_b.at[pl.ds(0, PEERS - 1)], asem)
        block = abuf_b[...].reshape(PEERS * 16, ROWS * LANES)
        plane = sum(
            pick(one, block[:, r * LANES : (r + 1) * LANES]) for r, one in enumerate(chosen)
        )
        plane = plane.astype(BF16)
        for s in range(SUBS):
            half = slice(s % 2 * LANES, (s % 2 + 1) * LANES)
            hb[z, s // 2, :, half] = plane[s * PLANE : (s + 1) * PLANE]
        b_step(0)

    load_targets.wait()
    for b in range(GROUPS):
        tcol[group(b), :] = to_column(targets[b : b + 1, :].astype(F32)).astype(jnp.int32)
    tsum[...] = jnp.zeros_like(tsum)
    offset = ((z * Y + y) * (X * C) + x * C + c) * COLS
    load_weight.wait()

    def spans(load):
        for ref, start in ((ha, 0), (hb, SPLIT)):
            for k in range(2):
                parts = [load(ref, q) for q in range(k * 4, (k + 1) * 4)]
                yield jnp.concatenate(parts, axis=1), start + k * 4 * UNIT, 4 * UNIT

    def compute(u):
        planes = [back(entry(WORK, u, k)) for k in range(2)]
        for p in planes:
            @pl.when(c == 0)
            def _():
                arrived(hb.at[p], csem.at[p])

            @pl.when(c == 1)
            def _():
                arrived(ha.at[p], csem.at[p])

        acc = jnp.zeros((2 * PLANE, COLS), F32)
        for parts, first, width in spans(lambda ref, q: jnp.concatenate([ref[p, q] for p in planes], axis=0)):
            acc += jnp.dot(parts, weight[first : first + width, :], preferred_element_type=F32)
        top = jnp.max(acc, axis=1, keepdims=True)
        e = jnp.exp(acc - top)
        lse = top + jnp.log(jnp.sum(e, axis=1, keepdims=True))
        ids = offset + lax.broadcasted_iota(jnp.int32, (PLANE, COLS), 1)
        for k, p in enumerate(planes):
            mine = slice(k * PLANE, (k + 1) * PLANE)
            rows = pl.ds(pl.multiple_of(p * PLANE, PLANE), PLANE)
            logits[rows, :] = acc[mine]
            mcol[rows, :] = top[mine]
            lcol[rows, :] = lse[mine]
            ebuf[rows, :] = e[mine].astype(BF16)
            send(ebuf.at[rows, :], pbuf.at[rows, :], out_sems.at[7], esem, copy=1 - copy)
            hit = jnp.where(ids == tcol[rows, :], acc[mine], 0.0)
            tsum[...] += jnp.sum(hit.reshape(PLANE // 8, 8, COLS), axis=0)

    def step(i, carry):
        @pl.when(c == 0)
        def _():
            a_step(i)

        @pl.when((c == 1) & (i > 0))
        def _():
            b_step(i)

        u = i - LAG + c

        @pl.when((u >= 0) & (u < STEPS))
        def _():
            compute(u)

        return carry

    lax.fori_loop(0, STEPS + LAG, step, 0)

    def to_plane(src, dst, sem_out, sem_in):
        def one(k, carry):
            send(src, dst.at[me], out_sems.at[sem_out], sem_in, **plane_peer(lax.rem(me + k, PEERS)))
            return carry

        lax.fori_loop(1, PEERS, one, 0)
        dst[pl.ds(me, 1)] = src[...][None]

    def to_line(src, dst, sem_out, sem_in):
        def one(k, carry):
            send(src, dst.at[z], out_sems.at[sem_out], sem_in, z=lax.rem(z + k, Z))
            return carry

        lax.fori_loop(1, Z, one, 0)
        dst[pl.ds(z, 1)] = src[...][None]

    def merged(parts):
        top = jnp.max(parts, axis=0)
        return top + jnp.log(jnp.sum(jnp.exp(parts - top[None]), axis=0))

    for b in range(GROUPS):
        lrow[b : b + 1, :] = to_row(lcol[group(b), :])
    to_plane(lrow, s1, 8, ssem.at[0])
    send(lrow, plrow, out_sems.at[9], ssem.at[1], copy=1 - copy)
    for b in range(GROUPS):
        mrow[b : b + 1, :] = to_row(mcol[group(b), :])
    send(mrow, pmrow, out_sems.at[10], ssem.at[2], copy=1 - copy)
    arrived(s1.at[pl.ds(0, PEERS - 1)], ssem.at[0])
    prow[...] = merged(s1[...])
    to_line(prow, s2, 11, ssem.at[3])

    arrived(plrow, ssem.at[1])
    arrived(pmrow, ssem.at[2])
    arrived(pbuf, esem)
    kmsg[...] = jnp.zeros_like(kmsg)
    for b in range(GROUPS):
        other = pbuf[group(b), :].astype(F32)
        apart = jnp.log(jnp.maximum(other, TINY)) - logits[group(b), :]
        weighted = jnp.sum(other * apart, axis=1, keepdims=True)
        mean = to_row(weighted / jnp.sum(other, axis=1, keepdims=True))
        kmsg[b : b + 1, :] = mean + pmrow[b : b + 1, :]
        kmsg[8 + b : 9 + b, :] = plrow[b : b + 1, :]
    hits = jnp.sum(tsum[...], axis=0, keepdims=True)
    kmsg[GROUPS : GROUPS + 1, :] = hits[:, :LANES] + hits[:, LANES:]
    to_plane(kmsg, k1, 12, ssem.at[4])

    arrived(k1.at[pl.ds(0, PEERS - 1)], ssem.at[4])
    plane_lse = k1[:, 8 : 8 + GROUPS, :]
    plrow_plane = merged(plane_lse)
    krow[...] = jnp.sum(jnp.exp(plane_lse - plrow_plane[None]) * k1[:, 0:GROUPS, :], axis=0)
    plrow[...] = plrow_plane
    line = lax.rem(me, GROUPS)
    zmsg[0:1, :] = plrow[pl.ds(line, 1), :]
    zmsg[1:2, :] = krow[pl.ds(line, 1), :]
    zmsg[2:3, :] = jnp.sum(k1[:, GROUPS : GROUPS + 1, :], axis=0)
    zmsg[3:4, :] = jnp.zeros((1, LANES), F32)
    to_line(zmsg, z1, 14, ssem.at[6])

    arrived(s2.at[pl.ds(0, Z - 1)], ssem.at[3])
    trow[...] = merged(s2[...])
    send(trow, ptrow, out_sems.at[13], ssem.at[5], copy=1 - copy)

    total = trow[...]
    ids = offset + lax.broadcasted_iota(jnp.int32, (LANES, COLS), 1)
    for b in range(GROUPS):
        probs = jnp.exp(logits[group(b), :] - to_column(total[b : b + 1, :]))
        hot = jnp.where(ids == tcol[group(b), :], 1.0, 0.0)
        logits[group(b), :] = (1.0 + DISTILL) * probs - hot
    arrived(z1.at[pl.ds(0, Z - 1)], ssem.at[6])
    line_lse = z1[:, 0:1, :]
    line_kl = z1[:, 1:2, :]
    lossv[...] = DISTILL * jnp.sum(jnp.exp(line_lse - merged(line_lse)[None]) * line_kl, axis=0)
    to_plane(lossv, l1, 16, ssem.at[7])

    arrived(ptrow, ssem.at[5])
    partner_total = ptrow[...]
    scale = DISTILL * jnp.exp(pmrow[...] - partner_total)
    for b in range(GROUPS):
        other = pbuf[group(b), :].astype(F32) * to_column(scale[b : b + 1, :])
        gt[:, group(b)] = (logits[group(b), :] - other).astype(BF16).T

    for block, first, width in spans(lambda ref, q: ref[:, q].reshape(TOKENS, -1)):
        rows = pl.ds(first, width)
        flipped = jnp.dot(gt[...], block, preferred_element_type=F32)
        obuf[rows, :] = flipped.astype(BF16).T
        pltpu.make_async_copy(obuf.at[rows, :], grad_hbm.at[rows, :], osem).start()

    arrived(l1.at[pl.ds(0, PEERS - 1)], ssem.at[7])
    per_token = (1.0 + DISTILL) * total - DISTILL * partner_total
    loss = jnp.sum(per_token) + jnp.sum(l1[0:GROUPS]) - jnp.sum(z1[:, 2:3, :])
    loss_ref[0] = loss * (1.0 / TOKENS)

    @pl.when(c == 0)
    def _():
        arrived(pad_a.at[pl.ds(0, CHIPS - 1)], out_sems.at[0])
        arrived(abuf_b.at[pl.ds(0, CHIPS)], out_sems.at[15])
        arrived(ha.at[pl.ds(0, Z - 1), 0], out_sems.at[1])
        arrived(ha.at[pl.ds(0, Z), 0], out_sems.at[2])
        arrived(ha.at[pl.ds(0, Z), pl.ds(0, Y * (X - 1))], out_sems.at[3])
        arrived(ha, out_sems.at[4])

    @pl.when(c == 1)
    def _():
        arrived(pad_a, out_sems.at[0])
        arrived(abuf_b.at[pl.ds(0, CHIPS - 1)], out_sems.at[15])
        arrived(hb, out_sems.at[5])
        arrived(hb.at[pl.ds(0, Z - 1)], out_sems.at[6])

    arrived(ebuf, out_sems.at[7])
    arrived(s1.at[pl.ds(0, PEERS - 1)], out_sems.at[8])
    arrived(lrow, out_sems.at[9])
    arrived(mrow, out_sems.at[10])
    arrived(s2.at[pl.ds(0, Z - 1)], out_sems.at[11])
    arrived(k1.at[pl.ds(0, PEERS - 1)], out_sems.at[12])
    arrived(trow, out_sems.at[13])
    arrived(z1.at[pl.ds(0, Z - 1)], out_sems.at[14])
    arrived(l1.at[pl.ds(0, PEERS - 1)], out_sems.at[16])
    arrived(obuf, osem)


def body(hidden, head_weight, targets):
    dma = pltpu.SemaphoreType.DMA
    stat = pltpu.VMEM((GROUPS, LANES), F32)
    hbm = pl.BlockSpec(memory_space=pltpu.HBM)
    grad, loss = pl.pallas_call(
        kernel,
        out_shape=(
            jax.ShapeDtypeStruct((D, COLS), BF16),
            jax.ShapeDtypeStruct((1,), F32),
        ),
        in_specs=[hbm, hbm, hbm],
        out_specs=(
            hbm,
            pl.BlockSpec(memory_space=pltpu.SMEM),
        ),
        scratch_shapes=[
            pltpu.VMEM((ROWS, D), BF16),
            pltpu.VMEM((GROUPS, LANES), jnp.int32),
            pltpu.VMEM((D, COLS), BF16),
            pltpu.VMEM((Z, CHIPS, PLANE, UNIT), BF16),
            pltpu.VMEM((Z, CHIPS, PLANE, UNIT), BF16),
            pltpu.VMEM((CHIPS, 16, LANES), F32),
            pltpu.VMEM((16, ROWS * LANES), F32),
            pltpu.VMEM((CHIPS, 16, LANES), BF16),
            pltpu.VMEM((16, ROWS * LANES), BF16),
            pltpu.VMEM((PEERS, 16, LANES), BF16),
            pltpu.VMEM((PEERS, 16, ROWS * LANES), BF16),
            pltpu.VMEM((TOKENS, COLS), F32),
            pltpu.VMEM((TOKENS, COLS), BF16),
            pltpu.VMEM((TOKENS, COLS), BF16),
            pltpu.VMEM((COLS, TOKENS), BF16),
            pltpu.VMEM((TOKENS, 1), jnp.int32),
            pltpu.VMEM((TOKENS, 1), F32),
            pltpu.VMEM((TOKENS, 1), F32),
            pltpu.VMEM((8, COLS), F32),
            stat,
            stat,
            stat,
            stat,
            pltpu.VMEM((PEERS, GROUPS, LANES), F32),
            stat,
            pltpu.VMEM((Z, GROUPS, LANES), F32),
            stat,
            stat,
            pltpu.VMEM((16, LANES), F32),
            pltpu.VMEM((PEERS, 16, LANES), F32),
            stat,
            pltpu.VMEM((4, LANES), F32),
            pltpu.VMEM((Z, 4, LANES), F32),
            pltpu.VMEM((1, LANES), F32),
            pltpu.VMEM((PEERS, 1, LANES), F32),
            pltpu.VMEM((D, COLS), BF16),
            dma,
            dma,
            dma,
            dma,
            dma((Z,)),
            dma((2, STEPS + 1, CHUNKS)),
            dma((Z,)),
            dma((X - 1, Z)),
            dma((Z,)),
            dma,
            dma((8,)),
            dma,
            pltpu.SemaphoreType.REGULAR((2,)),
            dma((17,)),
        ],
        compiler_params=pltpu.CompilerParams(
            collective_id=0, has_side_effects=True, vmem_limit_bytes=VMEM_BYTES
        ),
        cost_estimate=pl.CostEstimate(
            flops=4 * TOKENS * D * COLS,
            bytes_accessed=4 * D * COLS,
            transcendentals=3 * TOKENS * COLS,
        ),
    )(hidden, targets.reshape(GROUPS, LANES), head_weight[0])
    return grad[None], loss


def solution(mesh):
    torus = Mesh(
        mesh.devices.reshape(mesh.shape["copy"], Z, Y, X, C), ("copy", "z", "y", "x", "c")
    )
    everywhere = ("z", "y", "x", "c")
    in_specs = (P("copy", everywhere, None), P("copy", None, everywhere), P())
    out_specs = (P("copy", None, everywhere), P("copy"))
    return jax.shard_map(body, mesh=torus, in_specs=in_specs, out_specs=out_specs, check_vma=False)
```

```python
import jax
import jax.numpy as jnp
from jax import lax
from jax.experimental import pallas as pl
from jax.experimental.pallas import tpu as pltpu
from jax.sharding import Mesh
from jax.sharding import PartitionSpec as P

Z, Y, X, C = 16, 2, 4, 2
PEERS = Y * X * C
D = 4096
COLS = 256
ROWS = 3
PLANE = PEERS * ROWS
TOKENS = Z * PLANE
CHIPS = X * Y
UNIT = 256
SPLIT = CHIPS * UNIT
SUBS = 2 * CHIPS
CHUNKS = 4
STEPS = Z // 2
LAG = 3
WAIT = 3
LANES = 128
GROUPS = TOKENS // LANES
TINY = 1e-37
DISTILL = 0.5
VMEM_BYTES = 51 * 1024 * 1024

WORK = ((0, 1), (15, 2), (4, 12), (3, 13), (5, 11), (14, 6), (10, 7), (9, 8))

MESH = pl.DeviceIdType.MESH
F32 = jnp.float32
BF16 = jnp.bfloat16


def arrived(ref, sem):
    pltpu.make_async_copy(ref, ref, sem).wait()


def send(src, dst, send_sem, recv_sem, **where):
    pltpu.make_async_remote_copy(
        src_ref=src,
        dst_ref=dst,
        send_sem=send_sem,
        recv_sem=recv_sem,
        device_id=where,
        device_id_type=MESH,
    ).start()


def plane_peer(j):
    return {"y": j // (X * C), "x": lax.rem(j // C, X), "c": lax.rem(j, C)}


def kernel(
    hidden_hbm, targets_hbm, weight_hbm, grad_hbm, loss_ref,
    own_rows, targets, weight, ha, hb, stage_a, stage_b, pad_a, pad_b, abuf_a, abuf_b, logits, ebuf, pbuf, gt, tcol, mcol, lcol, kcol, tsum,
    lrow, mrow, plrow, pmrow, s1, prow, s2, trow, ptrow, kmsg, k1, krow, zmsg, z1, lossv, l1, obuf,
    wsem, hsem, tsem, asem, zsem_a, zsem_b, ysem, xsem, csem, esem, ssem, osem, near, out_sems,
):
    z, y, x, c = (lax.axis_index(n) for n in ("z", "y", "x", "c"))
    copy = lax.axis_index("copy")
    me = (y * X + x) * C + c
    unit = x * Y + y

    load_rows = pltpu.make_async_copy(hidden_hbm.at[0], own_rows, hsem)
    load_rows.start()

    def back(t):
        return lax.rem(z - t + Z, Z)

    def ahead(t):
        return lax.rem(z + t, Z)

    right, left = ahead(1), back(1)
    barrier = pltpu.get_barrier_semaphore()

    def meet(**where):
        pl.semaphore_signal(barrier, inc=1, device_id=where, device_id_type=MESH)

    def greet(k, carry):
        meet(**plane_peer(lax.rem(me + k, PEERS)))
        return carry

    meet(z=right)
    meet(z=left)
    meet(copy=1 - copy)
    lax.fori_loop(1, PEERS, greet, 0)

    load_targets = pltpu.make_async_copy(targets_hbm, targets, tsem)
    load_targets.start()
    load_weight = pltpu.make_async_copy(weight_hbm, weight, wsem)
    load_weight.start()

    stage_a[...] = jnp.zeros_like(stage_a)
    load_rows.wait()
    own = own_rows[...].astype(F32)
    for s in range(SUBS):
        for r in range(ROWS):
            half = own[r : r + 1, s * LANES : (s + 1) * LANES]
            stage_a[s // 2, 2 * r + s % 2 : 2 * r + s % 2 + 1, :] = half
            half = own[r : r + 1, SPLIT + s * LANES : SPLIT + (s + 1) * LANES]
            stage_b[s : s + 1, r * LANES : (r + 1) * LANES] = half
    pad_a[...] = stage_a[...].astype(BF16)
    pad_b[...] = stage_b[...].astype(BF16)

    pl.semaphore_wait(barrier, PEERS + 2)

    def give_first(y_to, x_to):
        send(
            pad_a.at[x_to * Y + y_to], abuf_a.at[me], out_sems.at[0], asem, y=y_to, x=x_to, c=0
        )

    def give_last(y_to, x_to):
        send(pad_b, abuf_b.at[me], out_sems.at[15], asem, y=y_to, x=x_to, c=1)

    def scatter(k, carry):
        chip = lax.rem(me // C + k, CHIPS)
        give_last(chip // X, lax.rem(chip, X))
        give_first(chip // X, lax.rem(chip, X))
        return carry

    lax.fori_loop(1, CHIPS, scatter, 0)

    @pl.when(c == 0)
    def _():
        give_last(y, x)
        abuf_a[pl.ds(me, 1)] = pad_a[pl.ds(unit, 1)]

    @pl.when(c == 1)
    def _():
        give_first(y, x)
        abuf_b[pl.ds(me, 1)] = pad_b[...][None]

    eye = lax.broadcasted_iota(jnp.int32, (LANES, LANES), 0) == lax.broadcasted_iota(
        jnp.int32, (LANES, LANES), 1
    )

    def to_row(column):
        return jnp.sum(jnp.where(eye, column, 0.0), axis=0, keepdims=True)

    def to_column(row):
        return jnp.sum(jnp.where(eye, row, 0.0), axis=1, keepdims=True)

    def group(b):
        return slice(b * LANES, (b + 1) * LANES)

    def selector(height, source):
        row = lax.broadcasted_iota(jnp.int32, (height, PEERS * 16), 0)
        col = lax.broadcasted_iota(jnp.int32, (1, PEERS * 16), 1)
        return jnp.where(row == source(col >> 4, col & 15), 1.0, 0.0).astype(BF16)

    def pick(chosen, block):
        return jnp.dot(chosen, block, preferred_element_type=F32)

    def move(ref, sem_out, sem_in, **where):
        send(ref, ref, out_sems.at[sem_out], sem_in, **where)

    def entry(table, t, k):
        digits = sum(pair[k] << (4 * n) for n, pair in enumerate(table[:7]))
        return jnp.where(t == 7, table[7][k], (digits >> (4 * jnp.minimum(t, 6))) & 15)

    def a_onward(p):
        for to in (right, left, ahead(2)):
            move(ha.at[p, unit], 1, zsem_a.at[p], z=to)

    def a_enter(p, further, opposite=False, known=False):
        ref = ha.at[p, unit]

        @pl.when((p != z) & jnp.logical_not(known))
        def _():
            arrived(ref, zsem_a.at[p])

        @pl.when(further)
        def _():
            a_onward(p)

        @pl.when(opposite)
        def _():
            move(ref, 1, zsem_a.at[p], z=ahead(4))

        move(ref, 2, ysem.at[p], y=1 - y)

    def a_second(p):
        arrived(ha.at[p, unit], ysem.at[p])
        ref = ha.at[p, pl.ds(x * Y, Y)]
        for k in range(1, X):
            move(ref, 3, xsem.at[k - 1, p], x=lax.rem(x + k, X))

    def a_third(p):
        for k in range(1, X):
            arrived(ha.at[p, pl.ds(lax.rem(x + X - k, X) * Y, Y)], xsem.at[k - 1, p])
        move(ha.at[p], 4, csem.at[p], c=1 - c)

    def a_step(i):
        @pl.when(i < STEPS)
        def _():
            a_enter(back(entry(WORK, i, 0)), i == 2, i == 2)
            a_enter(back(entry(WORK, i, 1)), i == 2, known=i == STEPS - 1)

        @pl.when(i == 3)
        def _():
            arrived(ha.at[back(8), unit], zsem_a.at[back(8)])
            a_onward(back(8))

        for lag, do in ((1, a_second), (3, a_third)):
            @pl.when((i >= lag) & (i < STEPS + lag))
            def _():
                for k in range(2):
                    do(back(entry(WORK, i - lag, k)))

    @pl.when(c == 0)
    def _():
        for distance in (1, 2):
            for p in (ahead(distance), back(distance)):
                pl.semaphore_signal(
                    near.at[distance - 1], inc=1, device_id={"z": p}, device_id_type=MESH
                )
            if distance == 1:
                pl.semaphore_wait(near.at[0], 2)
        chosen = []
        for h in range(2):
            def source(j, at, h=h):
                used = (at < 2 * ROWS) & ((at & 1) == h)
                return jnp.where(used, ROWS * j + (at >> 1), -1)

            chosen.append(selector(PLANE, source))
        arrived(abuf_a.at[pl.ds(0, PEERS - 1)], asem)
        block = abuf_a[...].reshape(PEERS * 16, LANES)
        halves = [pick(one, block) for one in chosen]
        ha[z, unit] = jnp.concatenate(halves, axis=1).astype(BF16)
        for p in (right, left):
            move(ha.at[z, unit], 1, zsem_a.at[z], z=p)
        pl.semaphore_wait(near.at[1], 2)
        for p in (ahead(4), back(4), ahead(2)):
            move(ha.at[z, unit], 1, zsem_a.at[z], z=p)

    def b_enter(p, t, direction, k):
        size = CHIPS // CHUNKS
        ref = hb.at[p, pl.ds(k * size, size)]

        @pl.when(t > 0)
        def _():
            arrived(ref, zsem_b.at[direction, t, k])

        @pl.when(t < STEPS - direction)
        def _():
            move(ref, 6, zsem_b.at[direction, t + 1, k], z=right if direction == 0 else left)

    def b_share(p):
        move(hb.at[p], 5, csem.at[p], c=1 - c)

    def b_step(i):
        for k in range(CHUNKS):
            @pl.when(i <= STEPS)
            def _():
                b_enter(back(i), i, 0, k)

            @pl.when(i < STEPS)
            def _():
                b_enter(ahead(i), i, 1, k)

        @pl.when(i <= STEPS)
        def _():
            b_share(back(i))

        @pl.when((i >= 1) & (i < STEPS))
        def _():
            b_share(ahead(i))

    @pl.when(c == 1)
    def _():
        chosen = [
            selector(SUBS * PLANE, lambda j, s, r=r: s * PLANE + ROWS * j + r) for r in range(ROWS)
        ]
        arrived(abuf_b.at[pl.ds(0, PEERS - 1)], asem)
        block = abuf_b[...].reshape(PEERS * 16, ROWS * LANES)
        plane = sum(
            pick(one, block[:, r * LANES : (r + 1) * LANES]) for r, one in enumerate(chosen)
        )
        plane = plane.astype(BF16)
        for s in range(SUBS):
            half = slice(s % 2 * LANES, (s % 2 + 1) * LANES)
            hb[z, s // 2, :, half] = plane[s * PLANE : (s + 1) * PLANE]
        b_step(0)

    load_targets.wait()
    for b in range(GROUPS):
        tcol[group(b), :] = to_column(targets[b : b + 1, :].astype(F32)).astype(jnp.int32)
    tsum[...] = jnp.zeros_like(tsum)
    offset = ((z * Y + y) * (X * C) + x * C + c) * COLS
    load_weight.wait()

    def spans(load):
        for ref, start in ((ha, 0), (hb, SPLIT)):
            for k in range(2):
                parts = [load(ref, q) for q in range(k * 4, (k + 1) * 4)]
                yield jnp.concatenate(parts, axis=1), start + k * 4 * UNIT, 4 * UNIT

    def compute(u):
        planes = [back(entry(WORK, u, k)) for k in range(2)]
        for p in planes:
            @pl.when(c == 0)
            def _():
                arrived(hb.at[p], csem.at[p])

            @pl.when(c == 1)
            def _():
                arrived(ha.at[p], csem.at[p])

        acc = jnp.zeros((2 * PLANE, COLS), F32)
        for parts, first, width in spans(lambda ref, q: jnp.concatenate([ref[p, q] for p in planes], axis=0)):
            acc += jnp.dot(parts, weight[first : first + width, :], preferred_element_type=F32)
        top = jnp.max(acc, axis=1, keepdims=True)
        e = jnp.exp(acc - top)
        lse = top + jnp.log(jnp.sum(e, axis=1, keepdims=True))
        ids = offset + lax.broadcasted_iota(jnp.int32, (PLANE, COLS), 1)
        for k, p in enumerate(planes):
            mine = slice(k * PLANE, (k + 1) * PLANE)
            rows = pl.ds(pl.multiple_of(p * PLANE, PLANE), PLANE)
            logits[rows, :] = acc[mine]
            mcol[rows, :] = top[mine]
            lcol[rows, :] = lse[mine]
            ebuf[rows, :] = e[mine].astype(BF16)
            send(ebuf.at[rows, :], pbuf.at[rows, :], out_sems.at[7], esem.at[p], copy=1 - copy)
            hit = jnp.where(ids == tcol[rows, :], acc[mine], 0.0)
            tsum[...] += jnp.sum(hit.reshape(PLANE // 8, 8, COLS), axis=0)

    def compare(u):
        for k in range(2):
            p = back(entry(WORK, u, k))
            rows = pl.ds(pl.multiple_of(p * PLANE, PLANE), PLANE)
            arrived(pbuf.at[rows, :], esem.at[p])
            other = pbuf[rows, :].astype(F32)
            apart = jnp.log(jnp.maximum(other, TINY)) - logits[rows, :]
            weighted = jnp.sum(other * apart, axis=1, keepdims=True)
            kcol[rows, :] = weighted / jnp.sum(other, axis=1, keepdims=True)

    def step(i, carry):
        @pl.when(c == 0)
        def _():
            a_step(i)

        @pl.when((c == 1) & (i > 0))
        def _():
            b_step(i)

        u = i - LAG

        @pl.when((u >= 0) & (u < STEPS))
        def _():
            compute(u)

        @pl.when(u >= WAIT)
        def _():
            compare(u - WAIT)

        return carry

    lax.fori_loop(0, STEPS + LAG, step, 0)

    def to_plane(src, dst, sem_out, sem_in):
        def one(k, carry):
            send(src, dst.at[me], out_sems.at[sem_out], sem_in, **plane_peer(lax.rem(me + k, PEERS)))
            return carry

        lax.fori_loop(1, PEERS, one, 0)
        dst[pl.ds(me, 1)] = src[...][None]

    def to_line(src, dst, sem_out, sem_in):
        def one(k, carry):
            send(src, dst.at[z], out_sems.at[sem_out], sem_in, z=lax.rem(z + k, Z))
            return carry

        lax.fori_loop(1, Z, one, 0)
        dst[pl.ds(z, 1)] = src[...][None]

    def merged(parts):
        top = jnp.max(parts, axis=0)
        return top + jnp.log(jnp.sum(jnp.exp(parts - top[None]), axis=0))

    for b in range(GROUPS):
        lrow[b : b + 1, :] = to_row(lcol[group(b), :])
    to_plane(lrow, s1, 8, ssem.at[0])
    send(lrow, plrow, out_sems.at[9], ssem.at[1], copy=1 - copy)
    for b in range(GROUPS):
        mrow[b : b + 1, :] = to_row(mcol[group(b), :])
    send(mrow, pmrow, out_sems.at[10], ssem.at[2], copy=1 - copy)
    arrived(s1.at[pl.ds(0, PEERS - 1)], ssem.at[0])
    prow[...] = merged(s1[...])
    to_line(prow, s2, 11, ssem.at[3])

    arrived(plrow, ssem.at[1])
    arrived(pmrow, ssem.at[2])
    for u in range(STEPS - WAIT, STEPS):
        compare(u)
    kmsg[...] = jnp.zeros_like(kmsg)
    for b in range(GROUPS):
        kmsg[b : b + 1, :] = to_row(kcol[group(b), :]) + pmrow[b : b + 1, :]
        kmsg[8 + b : 9 + b, :] = plrow[b : b + 1, :]
    hits = jnp.sum(tsum[...], axis=0, keepdims=True)
    kmsg[GROUPS : GROUPS + 1, :] = hits[:, :LANES] + hits[:, LANES:]
    to_plane(kmsg, k1, 12, ssem.at[4])

    arrived(k1.at[pl.ds(0, PEERS - 1)], ssem.at[4])
    plane_lse = k1[:, 8 : 8 + GROUPS, :]
    plrow_plane = merged(plane_lse)
    krow[...] = jnp.sum(jnp.exp(plane_lse - plrow_plane[None]) * k1[:, 0:GROUPS, :], axis=0)
    plrow[...] = plrow_plane
    line = lax.rem(me, GROUPS)
    zmsg[0:1, :] = plrow[pl.ds(line, 1), :]
    zmsg[1:2, :] = krow[pl.ds(line, 1), :]
    zmsg[2:3, :] = jnp.sum(k1[:, GROUPS : GROUPS + 1, :], axis=0)
    zmsg[3:4, :] = jnp.zeros((1, LANES), F32)
    to_line(zmsg, z1, 14, ssem.at[6])

    arrived(s2.at[pl.ds(0, Z - 1)], ssem.at[3])
    trow[...] = merged(s2[...])
    send(trow, ptrow, out_sems.at[13], ssem.at[5], copy=1 - copy)

    total = trow[...]
    ids = offset + lax.broadcasted_iota(jnp.int32, (LANES, COLS), 1)
    for b in range(GROUPS):
        probs = jnp.exp(logits[group(b), :] - to_column(total[b : b + 1, :]))
        hot = jnp.where(ids == tcol[group(b), :], 1.0, 0.0)
        logits[group(b), :] = (1.0 + DISTILL) * probs - hot
    arrived(z1.at[pl.ds(0, Z - 1)], ssem.at[6])
    line_lse = z1[:, 0:1, :]
    line_kl = z1[:, 1:2, :]
    lossv[...] = DISTILL * jnp.sum(jnp.exp(line_lse - merged(line_lse)[None]) * line_kl, axis=0)
    to_plane(lossv, l1, 16, ssem.at[7])

    arrived(ptrow, ssem.at[5])
    partner_total = ptrow[...]
    scale = DISTILL * jnp.exp(pmrow[...] - partner_total)
    for b in range(GROUPS):
        other = pbuf[group(b), :].astype(F32) * to_column(scale[b : b + 1, :])
        gt[:, group(b)] = (logits[group(b), :] - other).astype(BF16).T

    for block, first, width in spans(lambda ref, q: ref[:, q].reshape(TOKENS, -1)):
        rows = pl.ds(first, width)
        flipped = jnp.dot(gt[...], block, preferred_element_type=F32)
        obuf[rows, :] = flipped.astype(BF16).T
        pltpu.make_async_copy(obuf.at[rows, :], grad_hbm.at[rows, :], osem).start()

    arrived(l1.at[pl.ds(0, PEERS - 1)], ssem.at[7])
    per_token = (1.0 + DISTILL) * total - DISTILL * partner_total
    loss = jnp.sum(per_token) + jnp.sum(l1[0:GROUPS]) - jnp.sum(z1[:, 2:3, :])
    loss_ref[0] = loss * (1.0 / TOKENS)

    @pl.when(c == 0)
    def _():
        arrived(pad_a.at[pl.ds(0, CHIPS - 1)], out_sems.at[0])
        arrived(abuf_b.at[pl.ds(0, CHIPS)], out_sems.at[15])
        arrived(ha.at[pl.ds(0, Z - 1), 0], out_sems.at[1])
        arrived(ha.at[pl.ds(0, Z), 0], out_sems.at[2])
        arrived(ha.at[pl.ds(0, Z), pl.ds(0, Y * (X - 1))], out_sems.at[3])
        arrived(ha, out_sems.at[4])

    @pl.when(c == 1)
    def _():
        arrived(pad_a, out_sems.at[0])
        arrived(abuf_b.at[pl.ds(0, CHIPS - 1)], out_sems.at[15])
        arrived(hb, out_sems.at[5])
        arrived(hb.at[pl.ds(0, Z - 1)], out_sems.at[6])

    arrived(ebuf, out_sems.at[7])
    arrived(s1.at[pl.ds(0, PEERS - 1)], out_sems.at[8])
    arrived(lrow, out_sems.at[9])
    arrived(mrow, out_sems.at[10])
    arrived(s2.at[pl.ds(0, Z - 1)], out_sems.at[11])
    arrived(k1.at[pl.ds(0, PEERS - 1)], out_sems.at[12])
    arrived(trow, out_sems.at[13])
    arrived(z1.at[pl.ds(0, Z - 1)], out_sems.at[14])
    arrived(l1.at[pl.ds(0, PEERS - 1)], out_sems.at[16])
    arrived(obuf, osem)


def body(hidden, head_weight, targets):
    dma = pltpu.SemaphoreType.DMA
    stat = pltpu.VMEM((GROUPS, LANES), F32)
    hbm = pl.BlockSpec(memory_space=pltpu.HBM)
    grad, loss = pl.pallas_call(
        kernel,
        out_shape=(
            jax.ShapeDtypeStruct((D, COLS), BF16),
            jax.ShapeDtypeStruct((1,), F32),
        ),
        in_specs=[hbm, hbm, hbm],
        out_specs=(
            hbm,
            pl.BlockSpec(memory_space=pltpu.SMEM),
        ),
        scratch_shapes=[
            pltpu.VMEM((ROWS, D), BF16),
            pltpu.VMEM((GROUPS, LANES), jnp.int32),
            pltpu.VMEM((D, COLS), BF16),
            pltpu.VMEM((Z, CHIPS, PLANE, UNIT), BF16),
            pltpu.VMEM((Z, CHIPS, PLANE, UNIT), BF16),
            pltpu.VMEM((CHIPS, 16, LANES), F32),
            pltpu.VMEM((16, ROWS * LANES), F32),
            pltpu.VMEM((CHIPS, 16, LANES), BF16),
            pltpu.VMEM((16, ROWS * LANES), BF16),
            pltpu.VMEM((PEERS, 16, LANES), BF16),
            pltpu.VMEM((PEERS, 16, ROWS * LANES), BF16),
            pltpu.VMEM((TOKENS, COLS), F32),
            pltpu.VMEM((TOKENS, COLS), BF16),
            pltpu.VMEM((TOKENS, COLS), BF16),
            pltpu.VMEM((COLS, TOKENS), BF16),
            pltpu.VMEM((TOKENS, 1), jnp.int32),
            pltpu.VMEM((TOKENS, 1), F32),
            pltpu.VMEM((TOKENS, 1), F32),
            pltpu.VMEM((TOKENS, 1), F32),
            pltpu.VMEM((8, COLS), F32),
            stat,
            stat,
            stat,
            stat,
            pltpu.VMEM((PEERS, GROUPS, LANES), F32),
            stat,
            pltpu.VMEM((Z, GROUPS, LANES), F32),
            stat,
            stat,
            pltpu.VMEM((16, LANES), F32),
            pltpu.VMEM((PEERS, 16, LANES), F32),
            stat,
            pltpu.VMEM((4, LANES), F32),
            pltpu.VMEM((Z, 4, LANES), F32),
            pltpu.VMEM((1, LANES), F32),
            pltpu.VMEM((PEERS, 1, LANES), F32),
            pltpu.VMEM((D, COLS), BF16),
            dma,
            dma,
            dma,
            dma,
            dma((Z,)),
            dma((2, STEPS + 1, CHUNKS)),
            dma((Z,)),
            dma((X - 1, Z)),
            dma((Z,)),
            dma((Z,)),
            dma((8,)),
            dma,
            pltpu.SemaphoreType.REGULAR((2,)),
            dma((17,)),
        ],
        compiler_params=pltpu.CompilerParams(
            collective_id=0, has_side_effects=True, vmem_limit_bytes=VMEM_BYTES
        ),
        cost_estimate=pl.CostEstimate(
            flops=4 * TOKENS * D * COLS,
            bytes_accessed=4 * D * COLS,
            transcendentals=3 * TOKENS * COLS,
        ),
    )(hidden, targets.reshape(GROUPS, LANES), head_weight[0])
    return grad[None], loss


def solution(mesh):
    torus = Mesh(
        mesh.devices.reshape(mesh.shape["copy"], Z, Y, X, C), ("copy", "z", "y", "x", "c")
    )
    everywhere = ("z", "y", "x", "c")
    in_specs = (P("copy", everywhere, None), P("copy", None, everywhere), P())
    out_specs = (P("copy", None, everywhere), P("copy"))
    return jax.shard_map(body, mesh=torus, in_specs=in_specs, out_specs=out_specs, check_vma=False)
```
